32 devices in a mesh: sec: 4 (over z), row: 8 (over y, x, core).
Axes of the slice: x: 2, y: 2, z: 4, core: 2. Of those that a mesh axis runs over, the one named last changes fastest.
Arguments:
- image: float32 [16384, 4096], P(('sec', 'row')), parts along dimension 0, may hold values from -6 to 6
- cutoff: int32 [4], P('sec'), parts along dimension 0, may hold values from 512 to 1535
Outputs:
- filtered: float32 [16384, 4096], P(('sec', 'row')), parts along dimension 0
The draws below stay inside these ranges and needn't reach their ends.
There are 4 independent parts, one for each index of `sec`. The reference program is written for one: setup_inputs(seed, part) draws one part's arguments, and reference() takes and returns one part's arrays. A program takes and returns all parts, laid end to end along the dimension named above; each array names one. Nothing has to cross between parts.
All inputs are finite; a program needn't handle non-finite values.
Results may differ from the reference program's by a relative error of at most 0.00007.
Values sent between devices are 32-bit elements; how exact they have to be, the bound alone decides.
A program may use at most 128 MiB of HBM per device.

```python
import jax
import jax.numpy as jnp

NY = 4096
NX = 4096


def shard_levels(rng, extent, split, smallest, largest):
    level, own = 1.0, jax.random.fold_in(rng, 6)
    for position, shards_of in split:
        draws = jnp.exp(jax.random.uniform(jax.random.fold_in(own, position), (shards_of,), jnp.float32, smallest / len(split), largest / len(split)))
        level = level * jnp.repeat(draws, extent[position] // shards_of).reshape([-1 if axis == position else 1 for axis in range(len(extent))])
    return level


def gaussian(stream_key, shape, scale, bound, cuts=(), held_as=jnp.bfloat16):
    values = jax.random.normal(stream_key, shape, jnp.float32) * scale
    if len(cuts) > 0:
        values = shard_levels(stream_key, shape, cuts, -0.22, 0.18) * values
    return jnp.clip(values, min=-bound, max=bound).astype(held_as)


def setup_inputs(seed: int = 0, part: int = 0) -> dict:
    splits = jax.random.split(jax.random.key(seed), 3)
    part_splits = jax.random.split(jax.random.fold_in(splits[2], part), 3)
    return {
        "image": gaussian(part_splits[0], (NY, NX), 1.0, 6.0, ((0, 8),), jnp.float32),
        "cutoff": jax.random.randint(part_splits[1], (1,), NX // 8, 3 * NX // 8).astype(jnp.int32),
    }


def fold_index(total):
    positions = jnp.arange(total, dtype=jnp.int32)
    return jnp.minimum(positions, total - positions)


def reference(image, cutoff):
    spectrum = jnp.fft.fft2(image)
    row_freq = fold_index(NY)
    col_freq = fold_index(NX)
    radius = cutoff[0]
    passed = (row_freq[:, None] * row_freq[:, None] + col_freq[None, :] * col_freq[None, :]) >= radius * radius
    result = jnp.fft.ifft2(jnp.where(passed, spectrum, jnp.zeros_like(spectrum)))
    return jnp.real(result).astype(jnp.float32)
```

```python
import functools
import math

import jax
import jax.numpy as jnp
import ml_dtypes
import numpy as np
from jax import lax
from jax.experimental import pallas as pl
from jax.experimental.pallas import tpu as pltpu
from jax.sharding import PartitionSpec as P

RADIX = 16
UNITS = RADIX // 2
VMEM = 56 * 1024 * 1024


def turn(value, cosine, sine):
    real, imag = value
    if abs(sine) < 1e-12:
        return (real, imag) if cosine > 0 else (-real, -imag)
    if abs(cosine) < 1e-12:
        return (-imag, real) if sine > 0 else (imag, -real)
    if abs(abs(cosine) - abs(sine)) < 1e-12:
        first = real - imag if sine * cosine > 0 else real + imag
        second = real + imag if sine * cosine > 0 else imag - real
        return (first * cosine, second * cosine)
    return (real * cosine - imag * sine, real * sine + imag * cosine)


def plus(one, other):
    return (one[0] + other[0], one[1] + other[1])


def minus(one, other):
    return (one[0] - other[0], one[1] - other[1])


def complex_fft(values, sign):
    count = len(values)
    if count == 1:
        return values
    even = complex_fft(values[0::2], sign)
    odd = complex_fft(values[1::2], sign)
    low, high = [], []
    for k in range(count // 2):
        angle = sign * 2.0 * math.pi * k / count
        turned = turn(odd[k], math.cos(angle), math.sin(angle))
        low.append(plus(even[k], turned))
        high.append(minus(even[k], turned))
    return low + high


def real_fft(values):
    count = len(values)
    if count == 2:
        return [(values[0] + values[1], None), (values[0] - values[1], None)]
    even = real_fft(values[0::2])
    odd = real_fft(values[1::2])
    out = [None] * (count // 2 + 1)
    out[0] = (even[0][0] + odd[0][0], None)
    out[count // 2] = (even[0][0] - odd[0][0], None)
    quarter = count // 4
    out[quarter] = (even[quarter][0], -odd[quarter][0])
    for k in range(1, quarter):
        angle = -2.0 * math.pi * k / count
        turned = turn(odd[k], math.cos(angle), math.sin(angle))
        out[k] = plus(even[k], turned)
        lower = minus(even[k], turned)
        out[count // 2 - k] = (lower[0], -lower[1])
    return out


def real_inverse(values, count):
    if count == 2:
        return [values[0][0] + values[1][0], values[0][0] - values[1][0]]
    half, quarter = count // 2, count // 4
    even = [(values[0][0] + values[half][0], None)]
    odd = [(values[0][0] - values[half][0], None)]
    for k in range(1, quarter):
        mirror = (values[half - k][0], -values[half - k][1])
        even.append(plus(values[k], mirror))
        angle = 2.0 * math.pi * k / count
        odd.append(turn(minus(values[k], mirror), math.cos(angle), math.sin(angle)))
    even.append((2.0 * values[quarter][0], None))
    odd.append((-2.0 * values[quarter][1], None))
    even_out, odd_out = real_inverse(even, half), real_inverse(odd, half)
    return [item for pair in zip(even_out, odd_out) for item in pair]


def split(values):
    high = values.astype(jnp.bfloat16)
    return high, (values - high.astype(jnp.float32)).astype(jnp.bfloat16)


def table_halves(table):
    high = table.astype(np.float32).astype(ml_dtypes.bfloat16)
    low = (table - high.astype(np.float64)).astype(np.float32).astype(ml_dtypes.bfloat16)
    return np.stack([high, low])


def product(left, right, dims):
    def one(a, b):
        return lax.dot_general(a, b, dims, preferred_element_type=jnp.float32)

    return one(left[0], right[0]) + (one(left[0], right[1]) + one(left[1], right[0]))


def twiddles(length):
    chunk = length // RADIX
    angle = 2.0 * math.pi * np.outer(np.arange(RADIX), np.arange(chunk)) / length
    return np.stack([np.cos(angle), np.sin(angle)]).astype(np.float32)


def frequency_table(length, band):
    chunk, kept = length // RADIX, band // UNITS
    half = kept // 2
    inner = np.arange(chunk)[:, None]
    angle = 2.0 * math.pi * (inner * np.arange(-half, half)[None, :] % chunk) / chunk
    c, s = np.cos(angle), np.sin(angle)
    forward = np.block([[c, -s], [s, c]])
    inverse = np.concatenate([np.concatenate([c.T, s.T], 1), np.concatenate([-s.T, c.T], 1)], 0)
    angle0 = 2.0 * math.pi * (inner * (RADIX * np.arange(half))[None, :] % length) / length
    angle8 = 2.0 * math.pi * (inner * (UNITS + RADIX * np.arange(half))[None, :] % length) / length
    zero = np.zeros((chunk, half))
    forward0 = np.block(
        [[np.cos(angle0), zero, -np.sin(angle0), zero], [zero, np.cos(angle8), zero, -np.sin(angle8)]]
    )
    weight = np.full((half, 1), 2.0)
    weight[0, 0] = 1.0
    top = np.concatenate([weight * np.cos(angle0).T, zero.T], 1)
    second = np.concatenate([zero.T, 2.0 * np.cos(angle8).T], 1)
    third = np.concatenate([-weight * np.sin(angle0).T, zero.T], 1)
    fourth = np.concatenate([zero.T, -2.0 * np.sin(angle8).T], 1)
    inverse0 = np.concatenate([top, second, third, fourth], 0)
    return forward0, forward, inverse0, inverse


def rows_forward(image_ref, table_ref, tw_ref, out_ref, high_ref, low_ref):
    rows, length = image_ref.shape
    chunk = length // RADIX
    lanes = min(128, chunk)
    sub = 16

    def step(index, carry):
        at = pl.ds(pl.multiple_of(index * sub, sub), sub)
        for start in range(0, chunk, lanes):
            values = [image_ref[at, n * chunk + start : n * chunk + start + lanes] for n in range(RADIX)]
            freqs = real_fft(values)
            for unit in range(UNITS):
                if unit == 0:
                    pair = (freqs[0][0], freqs[UNITS][0])
                else:
                    real, imag = freqs[unit]
                    c = tw_ref[0, unit : unit + 1, start : start + lanes]
                    s = tw_ref[1, unit : unit + 1, start : start + lanes]
                    pair = (real * c + imag * s, imag * c - real * s)
                for part in range(2):
                    high, low = split(pair[part])
                    high_ref[unit, at, part * chunk + start : part * chunk + start + lanes] = high
                    low_ref[unit, at, part * chunk + start : part * chunk + start + lanes] = low
        return carry

    lax.fori_loop(0, rows // sub, step, 0)
    for unit in range(UNITS):
        which = min(unit, 1)
        out_ref[unit] = product(
            (table_ref[which, 0], table_ref[which, 1]),
            (high_ref[unit], low_ref[unit]),
            (((1,), (1,)), ((), ())),
        )


def columns_filter(scalar_ref, data_ref, fx2_ref, fy2_ref, fwd_ref, inv_ref, tw_ref, out_ref, work_ref):
    sources, _, cols, rows = data_ref.shape
    length = sources * rows
    chunk = length // RADIX
    lanes = min(128, chunk, rows)
    sub = 8

    def where_is(n, start):
        source, first = divmod(n * chunk + start, rows)
        return source, slice(first, first + lanes)

    def step_forward(index, carry):
        at = pl.ds(pl.multiple_of(index * sub, sub), sub)
        for start in range(0, chunk, lanes):
            values = []
            for n in range(RADIX):
                source, span = where_is(n, start)
                values.append((data_ref[source, 0, at, span], data_ref[source, 1, at, span]))
            for k, (real, imag) in enumerate(complex_fft(values, -1.0)):
                if k > 0:
                    c = tw_ref[0, k : k + 1, start : start + lanes]
                    s = tw_ref[1, k : k + 1, start : start + lanes]
                    real, imag = real * c + imag * s, imag * c - real * s
                work_ref[k, at, start : start + lanes] = real
                work_ref[k, at, chunk + start : chunk + start + lanes] = imag
        return carry

    lax.fori_loop(0, cols // sub, step_forward, 0)
    radius = scalar_ref[1]
    limit = radius * radius
    fx2 = fx2_ref[0, :, 0:1]
    dims = (((1,), (0,)), ((), ()))
    group = 4
    for k in range(0, RADIX, group):
        values = work_ref[k : k + group].reshape(group * cols, 2 * chunk)
        spectrum = product(split(values), (fwd_ref[0], fwd_ref[1]), dims)
        width = spectrum.shape[1]
        spectrum = spectrum.reshape(group, cols, width)
        fy2 = fy2_ref[k : k + group].reshape(group, 1, width)
        low = jnp.where(fx2[None] + fy2 < limit, spectrum, 0.0).reshape(group * cols, width)
        back = product(split(low), (inv_ref[0], inv_ref[1]), dims)
        work_ref[k : k + group] = back.reshape(group, cols, 2 * chunk)

    def step_inverse(index, carry):
        at = pl.ds(pl.multiple_of(index * sub, sub), sub)
        for start in range(0, chunk, lanes):
            values = []
            for k in range(RADIX):
                real = work_ref[k, at, start : start + lanes]
                imag = work_ref[k, at, chunk + start : chunk + start + lanes]
                if k > 0:
                    c = tw_ref[0, k : k + 1, start : start + lanes]
                    s = tw_ref[1, k : k + 1, start : start + lanes]
                    real, imag = real * c - imag * s, imag * c + real * s
                values.append((real, imag))
            for n, (real, imag) in enumerate(complex_fft(values, 1.0)):
                source, span = where_is(n, start)
                out_ref[source, 0, at, span] = real
                out_ref[source, 1, at, span] = imag
        return carry

    lax.fori_loop(0, cols // sub, step_inverse, 0)


def rows_inverse(data_ref, image_ref, table_ref, tw_ref, out_ref, work_ref):
    rows, length = image_ref.shape
    chunk = length // RADIX
    lanes = min(128, chunk)
    sub = 8
    for unit in range(UNITS):
        which = min(unit, 1)
        work_ref[unit] = product(
            split(data_ref[unit].T), (table_ref[which, 0], table_ref[which, 1]), (((1,), (0,)), ((), ()))
        )

    def step(index, carry):
        at = pl.ds(pl.multiple_of(index * sub, sub), sub)
        for start in range(0, chunk, lanes):
            freqs = [None] * (UNITS + 1)
            for unit in range(UNITS):
                real = work_ref[unit, at, start : start + lanes]
                imag = work_ref[unit, at, chunk + start : chunk + start + lanes]
                if unit == 0:
                    freqs[0], freqs[UNITS] = (real, None), (imag, None)
                else:
                    c = tw_ref[0, unit : unit + 1, start : start + lanes]
                    s = tw_ref[1, unit : unit + 1, start : start + lanes]
                    freqs[unit] = (real * c - imag * s, imag * c + real * s)
            for n, low in enumerate(real_inverse(freqs, RADIX)):
                span = slice(n * chunk + start, n * chunk + start + lanes)
                out_ref[at, span] = image_ref[at, span] - low
        return carry

    lax.fori_loop(0, rows // sub, step, 0)


def whole(shape):
    return pl.BlockSpec(shape, lambda *_: (0,) * len(shape))


def body(image, cutoff):
    rows_local, width = image.shape
    shards = lax.axis_size("row")
    position = lax.axis_index("row")
    height = rows_local * shards
    band = 3 * width // 8
    kept = band // UNITS
    half = kept // 2
    cols = band // shards
    per = shards // UNITS
    chunk = width // RADIX
    forward0, forward, inverse0, inverse = frequency_table(width, band)
    order = np.arange(2 * kept).reshape(2, per, cols).transpose(1, 0, 2).reshape(-1)
    row_forward = np.stack([table_halves(forward0.T[order]), table_halves(forward.T[order])])
    row_inverse = np.stack([table_halves(inverse0[order]), table_halves(inverse[order])])
    col_forward = table_halves(forward)
    col_inverse = table_halves(inverse / (width * height))
    tw = twiddles(width)
    steps = np.arange(-half, half)
    fy = np.arange(RADIX)[:, None] + RADIX * np.concatenate([steps, steps])[None, :]
    fy2 = (fy * fy).astype(np.int32)
    first = np.arange(half)
    fx = np.concatenate(
        [RADIX * first, UNITS + RADIX * first] + [unit + RADIX * steps for unit in range(1, UNITS)]
    )
    fx2 = np.broadcast_to((fx * fx).reshape(shards, cols, 1), (shards, cols, 128)).astype(np.int32)

    params = pltpu.CompilerParams(vmem_limit_bytes=VMEM)
    block = min(256, rows_local)
    spectrum = pl.pallas_call(
        rows_forward,
        grid=(rows_local // block,),
        out_shape=jax.ShapeDtypeStruct((UNITS, 2 * kept, rows_local), jnp.float32),
        in_specs=[
            pl.BlockSpec((block, width), lambda i: (i, 0)),
            whole(row_forward.shape),
            whole(tw.shape),
        ],
        out_specs=pl.BlockSpec((UNITS, 2 * kept, block), lambda i: (0, 0, i)),
        scratch_shapes=[pltpu.VMEM((UNITS, block, 2 * chunk), jnp.bfloat16)] * 2,
        compiler_params=params,
    )(image, row_forward, tw)
    columns = lax.all_to_all(
        spectrum.reshape(shards, 2 * cols, rows_local), "row", split_axis=0, concat_axis=0, tiled=True
    )
    part = math.gcd(cols, 32)
    scalars = jnp.stack([position.astype(jnp.int32), cutoff[0]])
    data_spec = pl.BlockSpec((shards, 2, part, rows_local), lambda i, s: (0, 0, i, 0))
    back = pl.pallas_call(
        columns_filter,
        grid_spec=pltpu.PrefetchScalarGridSpec(
            num_scalar_prefetch=1,
            grid=(cols // part,),
            in_specs=[
                data_spec,
                pl.BlockSpec((1, part, 128), lambda i, s: (s[0], i, 0)),
                whole(fy2.shape),
                whole(col_forward.shape),
                whole(col_inverse.shape),
                whole(tw.shape),
            ],
            out_specs=data_spec,
            scratch_shapes=[pltpu.VMEM((RADIX, part, 2 * chunk), jnp.float32)],
        ),
        out_shape=jax.ShapeDtypeStruct((shards, 2, cols, rows_local), jnp.float32),
        compiler_params=params,
    )(scalars, columns.reshape(shards, 2, cols, rows_local), fx2, fy2, col_forward, col_inverse, tw)
    returned = lax.all_to_all(
        back.reshape(shards, 2 * cols, rows_local), "row", split_axis=0, concat_axis=0, tiled=True
    )
    block = min(128, rows_local)
    return pl.pallas_call(
        rows_inverse,
        grid=(rows_local // block,),
        out_shape=jax.ShapeDtypeStruct((rows_local, width), jnp.float32),
        in_specs=[
            pl.BlockSpec((UNITS, 2 * kept, block), lambda i: (0, 0, i)),
            pl.BlockSpec((block, width), lambda i: (i, 0)),
            whole(row_inverse.shape),
            whole(tw.shape),
        ],
        out_specs=pl.BlockSpec((block, width), lambda i: (i, 0)),
        scratch_shapes=[pltpu.VMEM((UNITS, block, 2 * chunk), jnp.float32)],
        compiler_params=params,
    )(returned.reshape(UNITS, 2 * kept, rows_local), image, row_inverse, tw)


def solution(mesh):
    return jax.shard_map(
        body,
        mesh=mesh,
        in_specs=(P(("sec", "row"), None), P("sec")),
        out_specs=P(("sec", "row"), None),
        check_vma=False,
    )
```

```python
import functools
import math

import jax
import jax.numpy as jnp
import ml_dtypes
import numpy as np
from jax import lax
from jax.experimental import pallas as pl
from jax.experimental.pallas import tpu as pltpu
from jax.sharding import PartitionSpec as P

RADIX = 16
UNITS = RADIX // 2
VMEM = 56 * 1024 * 1024


def turn(value, cosine, sine):
    real, imag = value
    if abs(sine) < 1e-12:
        return (real, imag) if cosine > 0 else (-real, -imag)
    if abs(cosine) < 1e-12:
        return (-imag, real) if sine > 0 else (imag, -real)
    if abs(abs(cosine) - abs(sine)) < 1e-12:
        first = real - imag if sine * cosine > 0 else real + imag
        second = real + imag if sine * cosine > 0 else imag - real
        return (first * cosine, second * cosine)
    return (real * cosine - imag * sine, real * sine + imag * cosine)


def plus(one, other):
    return (one[0] + other[0], one[1] + other[1])


def minus(one, other):
    return (one[0] - other[0], one[1] - other[1])


def complex_fft(values, sign):
    count = len(values)
    if count == 1:
        return values
    even = complex_fft(values[0::2], sign)
    odd = complex_fft(values[1::2], sign)
    low, high = [], []
    for k in range(count // 2):
        angle = sign * 2.0 * math.pi * k / count
        turned = turn(odd[k], math.cos(angle), math.sin(angle))
        low.append(plus(even[k], turned))
        high.append(minus(even[k], turned))
    return low + high


def real_fft(values):
    count = len(values)
    if count == 2:
        return [(values[0] + values[1], None), (values[0] - values[1], None)]
    even = real_fft(values[0::2])
    odd = real_fft(values[1::2])
    out = [None] * (count // 2 + 1)
    out[0] = (even[0][0] + odd[0][0], None)
    out[count // 2] = (even[0][0] - odd[0][0], None)
    quarter = count // 4
    out[quarter] = (even[quarter][0], -odd[quarter][0])
    for k in range(1, quarter):
        angle = -2.0 * math.pi * k / count
        turned = turn(odd[k], math.cos(angle), math.sin(angle))
        out[k] = plus(even[k], turned)
        lower = minus(even[k], turned)
        out[count // 2 - k] = (lower[0], -lower[1])
    return out


def real_inverse(values, count):
    if count == 2:
        return [values[0][0] + values[1][0], values[0][0] - values[1][0]]
    half, quarter = count // 2, count // 4
    even = [(values[0][0] + values[half][0], None)]
    odd = [(values[0][0] - values[half][0], None)]
    for k in range(1, quarter):
        mirror = (values[half - k][0], -values[half - k][1])
        even.append(plus(values[k], mirror))
        angle = 2.0 * math.pi * k / count
        odd.append(turn(minus(values[k], mirror), math.cos(angle), math.sin(angle)))
    even.append((2.0 * values[quarter][0], None))
    odd.append((-2.0 * values[quarter][1], None))
    even_out, odd_out = real_inverse(even, half), real_inverse(odd, half)
    return [item for pair in zip(even_out, odd_out) for item in pair]


def split(values):
    high = values.astype(jnp.bfloat16)
    return high, (values - high.astype(jnp.float32)).astype(jnp.bfloat16)


def table_halves(table):
    high = table.astype(np.float32).astype(ml_dtypes.bfloat16)
    low = (table - high.astype(np.float64)).astype(np.float32).astype(ml_dtypes.bfloat16)
    return np.stack([high, low])


def product(left, right, dims):
    def one(a, b):
        return lax.dot_general(a, b, dims, preferred_element_type=jnp.float32)

    return one(left[0], right[0]) + (one(left[0], right[1]) + one(left[1], right[0]))


def twiddles(length):
    chunk = length // RADIX
    angle = 2.0 * math.pi * np.outer(np.arange(RADIX), np.arange(chunk)) / length
    return np.stack([np.cos(angle), np.sin(angle)]).astype(np.float32)


def frequency_table(length, band):
    chunk, kept = length // RADIX, band // UNITS
    half = kept // 2
    inner = np.arange(chunk)[:, None]
    angle = 2.0 * math.pi * (inner * np.arange(-half, half)[None, :] % chunk) / chunk
    c, s = np.cos(angle), np.sin(angle)
    forward = np.block([[c, -s], [s, c]])
    inverse = np.concatenate([np.concatenate([c.T, s.T], 1), np.concatenate([-s.T, c.T], 1)], 0)
    angle0 = 2.0 * math.pi * (inner * (RADIX * np.arange(half))[None, :] % length) / length
    angle8 = 2.0 * math.pi * (inner * (UNITS + RADIX * np.arange(half))[None, :] % length) / length
    zero = np.zeros((chunk, half))
    forward0 = np.block(
        [[np.cos(angle0), zero, -np.sin(angle0), zero], [zero, np.cos(angle8), zero, -np.sin(angle8)]]
    )
    weight = np.full((half, 1), 2.0)
    weight[0, 0] = 1.0
    top = np.concatenate([weight * np.cos(angle0).T, zero.T], 1)
    second = np.concatenate([zero.T, 2.0 * np.cos(angle8).T], 1)
    third = np.concatenate([-weight * np.sin(angle0).T, zero.T], 1)
    fourth = np.concatenate([zero.T, -2.0 * np.sin(angle8).T], 1)
    inverse0 = np.concatenate([top, second, third, fourth], 0)
    return forward0, forward, inverse0, inverse


def rows_forward(image_ref, tw_ref, high_ref, low_ref):
    rows, length = image_ref.shape
    chunk = length // RADIX
    lanes = min(128, chunk)
    sub = 16

    def step(index, carry):
        at = pl.ds(pl.multiple_of(index * sub, sub), sub)
        for start in range(0, chunk, lanes):
            values = [image_ref[at, n * chunk + start : n * chunk + start + lanes] for n in range(RADIX)]
            freqs = real_fft(values)
            for unit in range(UNITS):
                if unit == 0:
                    pair = (freqs[0][0], freqs[UNITS][0])
                else:
                    real, imag = freqs[unit]
                    c = tw_ref[0, unit : unit + 1, start : start + lanes]
                    s = tw_ref[1, unit : unit + 1, start : start + lanes]
                    pair = (real * c + imag * s, imag * c - real * s)
                for part in range(2):
                    high, low = split(pair[part])
                    high_ref[unit, at, part * chunk + start : part * chunk + start + lanes] = high
                    low_ref[unit, at, part * chunk + start : part * chunk + start + lanes] = low
        return carry

    lax.fori_loop(0, rows // sub, step, 0)


def columns_filter(group, position, cutoff_ref, data_ref, fx2_ref, fy2_ref, fwd_ref, inv_ref, tw_ref, out_ref, work_ref):
    _, sources, _, cols, rows = data_ref.shape
    length = sources * rows
    chunk = length // RADIX
    lanes = min(128, chunk, rows)
    sub = 8

    def where_is(n, start):
        source, first = divmod(n * chunk + start, rows)
        return source, slice(first, first + lanes)

    def step_forward(index, carry):
        at = pl.ds(pl.multiple_of(index * sub, sub), sub)
        for start in range(0, chunk, lanes):
            values = []
            for n in range(RADIX):
                source, span = where_is(n, start)
                values.append((data_ref[group, source, 0, at, span], data_ref[group, source, 1, at, span]))
            for k, (real, imag) in enumerate(complex_fft(values, -1.0)):
                if k > 0:
                    c = tw_ref[0, k : k + 1, start : start + lanes]
                    s = tw_ref[1, k : k + 1, start : start + lanes]
                    real, imag = real * c + imag * s, imag * c - real * s
                work_ref[k, at, start : start + lanes] = real
                work_ref[k, at, chunk + start : chunk + start + lanes] = imag
        return carry

    lax.fori_loop(0, cols // sub, step_forward, 0)
    radius = cutoff_ref[0]
    limit = radius * radius
    fx2 = fx2_ref[position, group, :, 0:1]
    dims = (((1,), (0,)), ((), ()))
    batch = 4

    def step_matmul(index, carry):
        span = pl.ds(index * batch, batch)
        values = work_ref[span].reshape(batch * cols, 2 * chunk)
        spectrum = product(split(values), (fwd_ref[0], fwd_ref[1]), dims)
        width = spectrum.shape[1]
        spectrum = spectrum.reshape(batch, cols, width)
        fy2 = fy2_ref[span]
        low = jnp.where(fx2[None] + fy2 < limit, spectrum, 0.0).reshape(batch * cols, width)
        back = product(split(low), (inv_ref[0], inv_ref[1]), dims)
        work_ref[span] = back.reshape(batch, cols, 2 * chunk)
        return carry

    lax.fori_loop(0, RADIX // batch, step_matmul, 0)

    def step_inverse(index, carry):
        at = pl.ds(pl.multiple_of(index * sub, sub), sub)
        for start in range(0, chunk, lanes):
            values = []
            for k in range(RADIX):
                real = work_ref[k, at, start : start + lanes]
                imag = work_ref[k, at, chunk + start : chunk + start + lanes]
                if k > 0:
                    c = tw_ref[0, k : k + 1, start : start + lanes]
                    s = tw_ref[1, k : k + 1, start : start + lanes]
                    real, imag = real * c - imag * s, imag * c + real * s
                values.append((real, imag))
            for n, (real, imag) in enumerate(complex_fft(values, 1.0)):
                source, span = where_is(n, start)
                out_ref[group, source, 0, at, span] = real
                out_ref[group, source, 1, at, span] = imag
        return carry

    lax.fori_loop(0, cols // sub, step_inverse, 0)


def exchange(
    shards, cutoff_ref, image_ref, row_ref, tw_ref, fx2_ref, fy2_ref, fwd_ref, inv_ref, out_ref,
    high_ref, low_ref, sent_ref, held_ref, work_ref, back_ref, send_sem, recv_sem, back_send, back_recv, own_sem,
):
    groups, _, _, cols, rows = held_ref.shape
    per = shards // UNITS
    me = lax.axis_index("row")

    def partner(step):
        return lax.rem(me + step, shards)

    def forward_copy(group, step):
        dest = partner(step)
        return pltpu.make_async_remote_copy(
            src_ref=sent_ref.at[step, group],
            dst_ref=held_ref.at[group, me],
            send_sem=send_sem.at[group, step],
            recv_sem=recv_sem.at[group, step],
            device_id={"row": dest},
            device_id_type=pl.DeviceIdType.MESH,
        )

    def back_copy(group, step):
        dest = partner(step)
        return pltpu.make_async_remote_copy(
            src_ref=back_ref.at[group, dest],
            dst_ref=out_ref.at[me, group],
            send_sem=back_send.at[group, step],
            recv_sem=back_recv.at[group, step],
            device_id={"row": dest},
            device_id_type=pl.DeviceIdType.MESH,
        )

    def own_copy(group):
        return pltpu.make_async_copy(back_ref.at[group, me], out_ref.at[me, group], own_sem.at[group])

    def every(function):
        def loop(step, carry):
            function(step)
            return carry

        lax.fori_loop(1, shards, loop, 0)

    barrier = pltpu.get_barrier_semaphore()
    every(
        lambda step: pl.semaphore_signal(
            barrier, inc=1, device_id={"row": partner(step)}, device_id_type=pl.DeviceIdType.MESH
        )
    )
    rows_forward(image_ref, tw_ref, high_ref, low_ref)
    pl.semaphore_wait(barrier, shards - 1)

    def columns_of(dest):
        unit, part = dest // per, lax.rem(dest, per)
        which = jnp.minimum(unit, 1)
        values = product(
            (row_ref[which, 0, part], row_ref[which, 1, part]),
            (high_ref[unit], low_ref[unit]),
            (((1,), (1,)), ((), ())),
        )
        return values.reshape(groups, 2, cols, rows)

    def produce(step):
        sent_ref[step] = columns_of(partner(step))
        forward_copy(0, step).start()

    every(produce)
    for group in range(1, groups):
        every(lambda step: forward_copy(group, step).start())
    own = columns_of(me)
    for group in range(groups):
        held_ref[group, me] = own[group]

    def filter_group(group, carry):
        every(lambda step: forward_copy(group, step).wait_recv())
        columns_filter(
            group, me, cutoff_ref, held_ref, fx2_ref, fy2_ref, fwd_ref, inv_ref, tw_ref, back_ref, work_ref
        )
        every(lambda step: back_copy(group, step).start())
        own_copy(group).start()
        return carry

    lax.fori_loop(0, groups, filter_group, 0)

    def finish(group, carry):
        every(lambda step: forward_copy(group, step).wait_send())
        every(lambda step: back_copy(group, step).wait())
        own_copy(group).wait()
        return carry

    lax.fori_loop(0, groups, finish, 0)


def rows_inverse(data_ref, image_ref, table_ref, tw_ref, out_ref, work_ref):
    rows, length = image_ref.shape
    chunk = length // RADIX
    lanes = min(128, chunk)
    sub = 8
    for unit in range(UNITS):
        which = min(unit, 1)
        work_ref[unit] = product(
            split(data_ref[unit].T), (table_ref[which, 0], table_ref[which, 1]), (((1,), (0,)), ((), ()))
        )

    def step(index, carry):
        at = pl.ds(pl.multiple_of(index * sub, sub), sub)
        for start in range(0, chunk, lanes):
            freqs = [None] * (UNITS + 1)
            for unit in range(UNITS):
                real = work_ref[unit, at, start : start + lanes]
                imag = work_ref[unit, at, chunk + start : chunk + start + lanes]
                if unit == 0:
                    freqs[0], freqs[UNITS] = (real, None), (imag, None)
                else:
                    c = tw_ref[0, unit : unit + 1, start : start + lanes]
                    s = tw_ref[1, unit : unit + 1, start : start + lanes]
                    freqs[unit] = (real * c - imag * s, imag * c + real * s)
            for n, low in enumerate(real_inverse(freqs, RADIX)):
                span = slice(n * chunk + start, n * chunk + start + lanes)
                out_ref[at, span] = image_ref[at, span] - low
        return carry

    lax.fori_loop(0, rows // sub, step, 0)


def whole(shape):
    return pl.BlockSpec(shape, lambda *_: (0,) * len(shape))


def body(image, cutoff):
    rows_local, width = image.shape
    shards = lax.axis_size("row")
    height = rows_local * shards
    band = 3 * width // 8
    kept = band // UNITS
    half = kept // 2
    cols = band // shards
    per = shards // UNITS
    chunk = width // RADIX
    forward0, forward, inverse0, inverse = frequency_table(width, band)
    part = math.gcd(cols, 64)
    groups = cols // part
    order = np.arange(2 * kept).reshape(2, per, groups, part).transpose(1, 2, 0, 3).reshape(-1)
    row_forward = np.stack([table_halves(forward0.T[order]), table_halves(forward.T[order])])
    row_forward = row_forward.reshape(2, 2, per, 2 * cols, 2 * chunk)
    row_inverse = np.stack([table_halves(inverse0[order]), table_halves(inverse[order])])
    col_forward = table_halves(forward)
    col_inverse = table_halves(inverse / (width * height))
    tw = twiddles(width)
    steps = np.arange(-half, half)
    fy = np.arange(RADIX)[:, None] + RADIX * np.concatenate([steps, steps])[None, :]
    fy2 = (fy * fy).astype(np.int32)[:, None, :]
    first = np.arange(half)
    fx = np.concatenate(
        [RADIX * first, UNITS + RADIX * first] + [unit + RADIX * steps for unit in range(1, UNITS)]
    )
    fx2 = np.broadcast_to((fx * fx).reshape(shards, groups, part, 1), (shards, groups, part, 128)).astype(np.int32)

    vmem = pl.BlockSpec(memory_space=pltpu.VMEM)
    returned = pl.pallas_call(
        functools.partial(exchange, shards),
        out_shape=jax.ShapeDtypeStruct((shards, groups, 2, part, rows_local), jnp.float32),
        in_specs=[pl.BlockSpec(memory_space=pltpu.SMEM)] + [vmem] * 7,
        out_specs=pl.BlockSpec(memory_space=pl.ANY),
        scratch_shapes=[
            pltpu.VMEM((UNITS, rows_local, 2 * chunk), jnp.bfloat16),
            pltpu.VMEM((UNITS, rows_local, 2 * chunk), jnp.bfloat16),
            pltpu.VMEM((shards, groups, 2, part, rows_local), jnp.float32),
            pltpu.VMEM((groups, shards, 2, part, rows_local), jnp.float32),
            pltpu.VMEM((RADIX, part, 2 * chunk), jnp.float32),
            pltpu.VMEM((groups, shards, 2, part, rows_local), jnp.float32),
            pltpu.SemaphoreType.DMA((groups, shards)),
            pltpu.SemaphoreType.DMA((groups, shards)),
            pltpu.SemaphoreType.DMA((groups, shards)),
            pltpu.SemaphoreType.DMA((groups, shards)),
            pltpu.SemaphoreType.DMA((groups,)),
        ],
        compiler_params=pltpu.CompilerParams(
            vmem_limit_bytes=VMEM, collective_id=0, has_side_effects=True
        ),
    )(cutoff, image, row_forward, tw, fx2, fy2, col_forward, col_inverse)
    params = pltpu.CompilerParams(vmem_limit_bytes=VMEM)
    block = min(128, rows_local)
    return pl.pallas_call(
        rows_inverse,
        grid=(rows_local // block,),
        out_shape=jax.ShapeDtypeStruct((rows_local, width), jnp.float32),
        in_specs=[
            pl.BlockSpec((UNITS, 2 * kept, block), lambda i: (0, 0, i)),
            pl.BlockSpec((block, width), lambda i: (i, 0)),
            whole(row_inverse.shape),
            whole(tw.shape),
        ],
        out_specs=pl.BlockSpec((block, width), lambda i: (i, 0)),
        scratch_shapes=[pltpu.VMEM((UNITS, block, 2 * chunk), jnp.float32)],
        compiler_params=params,
    )(returned.reshape(UNITS, 2 * kept, rows_local), image, row_inverse, tw)


def solution(mesh):
    return jax.shard_map(
        body,
        mesh=mesh,
        in_specs=(P(("sec", "row"), None), P("sec")),
        out_specs=P(("sec", "row"), None),
        check_vma=False,
    )
```

```python
import functools
import math

import jax
import jax.numpy as jnp
import ml_dtypes
import numpy as np
from jax import lax
from jax.experimental import pallas as pl
from jax.experimental.pallas import tpu as pltpu
from jax.sharding import PartitionSpec as P

RADIX = 16
UNITS = RADIX // 2
VMEM = 56 * 1024 * 1024


def turn(value, cosine, sine):
    real, imag = value
    if abs(sine) < 1e-12:
        return (real, imag) if cosine > 0 else (-real, -imag)
    if abs(cosine) < 1e-12:
        return (-imag, real) if sine > 0 else (imag, -real)
    if abs(abs(cosine) - abs(sine)) < 1e-12:
        first = real - imag if sine * cosine > 0 else real + imag
        second = real + imag if sine * cosine > 0 else imag - real
        return (first * cosine, second * cosine)
    return (real * cosine - imag * sine, real * sine + imag * cosine)


def plus(one, other):
    return (one[0] + other[0], one[1] + other[1])


def minus(one, other):
    return (one[0] - other[0], one[1] - other[1])


def complex_fft(values, sign):
    count = len(values)
    if count == 1:
        return values
    even = complex_fft(values[0::2], sign)
    odd = complex_fft(values[1::2], sign)
    low, high = [], []
    for k in range(count // 2):
        angle = sign * 2.0 * math.pi * k / count
        turned = turn(odd[k], math.cos(angle), math.sin(angle))
        low.append(plus(even[k], turned))
        high.append(minus(even[k], turned))
    return low + high


def real_fft(values):
    count = len(values)
    if count == 2:
        return [(values[0] + values[1], None), (values[0] - values[1], None)]
    even = real_fft(values[0::2])
    odd = real_fft(values[1::2])
    out = [None] * (count // 2 + 1)
    out[0] = (even[0][0] + odd[0][0], None)
    out[count // 2] = (even[0][0] - odd[0][0], None)
    quarter = count // 4
    out[quarter] = (even[quarter][0], -odd[quarter][0])
    for k in range(1, quarter):
        angle = -2.0 * math.pi * k / count
        turned = turn(odd[k], math.cos(angle), math.sin(angle))
        out[k] = plus(even[k], turned)
        lower = minus(even[k], turned)
        out[count // 2 - k] = (lower[0], -lower[1])
    return out


def real_inverse(values, count):
    if count == 2:
        return [values[0][0] + values[1][0], values[0][0] - values[1][0]]
    half, quarter = count // 2, count // 4
    even = [(values[0][0] + values[half][0], None)]
    odd = [(values[0][0] - values[half][0], None)]
    for k in range(1, quarter):
        mirror = (values[half - k][0], -values[half - k][1])
        even.append(plus(values[k], mirror))
        angle = 2.0 * math.pi * k / count
        odd.append(turn(minus(values[k], mirror), math.cos(angle), math.sin(angle)))
    even.append((2.0 * values[quarter][0], None))
    odd.append((-2.0 * values[quarter][1], None))
    even_out, odd_out = real_inverse(even, half), real_inverse(odd, half)
    return [item for pair in zip(even_out, odd_out) for item in pair]


def split(values):
    high = values.astype(jnp.bfloat16)
    return high, (values - high.astype(jnp.float32)).astype(jnp.bfloat16)


def table_halves(table):
    high = table.astype(np.float32).astype(ml_dtypes.bfloat16)
    low = (table - high.astype(np.float64)).astype(np.float32).astype(ml_dtypes.bfloat16)
    return np.stack([high, low])


def product(left, right, dims):
    def one(a, b):
        return lax.dot_general(a, b, dims, preferred_element_type=jnp.float32)

    return one(left[0], right[0]) + (one(left[0], right[1]) + one(left[1], right[0]))


def twiddles(length):
    chunk = length // RADIX
    angle = 2.0 * math.pi * np.outer(np.arange(RADIX), np.arange(chunk)) / length
    return np.stack([np.cos(angle), np.sin(angle)]).astype(np.float32)


def frequency_table(length, band):
    chunk, kept = length // RADIX, band // UNITS
    half = kept // 2
    inner = np.arange(chunk)[:, None]
    angle = 2.0 * math.pi * (inner * np.arange(-half, half)[None, :] % chunk) / chunk
    c, s = np.cos(angle), np.sin(angle)
    forward = np.block([[c, -s], [s, c]])
    inverse = np.concatenate([np.concatenate([c.T, s.T], 1), np.concatenate([-s.T, c.T], 1)], 0)
    angle0 = 2.0 * math.pi * (inner * (RADIX * np.arange(half))[None, :] % length) / length
    angle8 = 2.0 * math.pi * (inner * (UNITS + RADIX * np.arange(half))[None, :] % length) / length
    zero = np.zeros((chunk, half))
    forward0 = np.block(
        [[np.cos(angle0), zero, -np.sin(angle0), zero], [zero, np.cos(angle8), zero, -np.sin(angle8)]]
    )
    weight = np.full((half, 1), 2.0)
    weight[0, 0] = 1.0
    top = np.concatenate([weight * np.cos(angle0).T, zero.T], 1)
    second = np.concatenate([zero.T, 2.0 * np.cos(angle8).T], 1)
    third = np.concatenate([-weight * np.sin(angle0).T, zero.T], 1)
    fourth = np.concatenate([zero.T, -2.0 * np.sin(angle8).T], 1)
    inverse0 = np.concatenate([top, second, third, fourth], 0)
    return forward0, forward, inverse0, inverse


def rows_forward(image_ref, slab_copy, slabs, tw_ref, high_ref, low_ref):
    rows, length = image_ref.shape
    chunk = length // RADIX
    lanes = min(128, chunk)
    sub = 16

    def step(index, carry):
        at = pl.ds(pl.multiple_of(index * sub, sub), sub)
        for start in range(0, chunk, lanes):
            values = [image_ref[at, n * chunk + start : n * chunk + start + lanes] for n in range(RADIX)]
            freqs = real_fft(values)
            for unit in range(UNITS):
                if unit == 0:
                    pair = (freqs[0][0], freqs[UNITS][0])
                else:
                    real, imag = freqs[unit]
                    c = tw_ref[0, unit : unit + 1, start : start + lanes]
                    s = tw_ref[1, unit : unit + 1, start : start + lanes]
                    pair = (real * c + imag * s, imag * c - real * s)
                for part in range(2):
                    high, low = split(pair[part])
                    high_ref[unit, at, part * chunk + start : part * chunk + start + lanes] = high
                    low_ref[unit, at, part * chunk + start : part * chunk + start + lanes] = low
        return carry

    count = rows // sub // slabs
    for slab in range(slabs):
        slab_copy(slab).wait()
        lax.fori_loop(slab * count, (slab + 1) * count, step, 0)


def columns_filter(group, position, cutoff_ref, data_ref, fx2_ref, fy2_ref, fwd_ref, inv_ref, tw_ref, out_ref, work_ref):
    _, sources, _, cols, rows = data_ref.shape
    length = sources * rows
    chunk = length // RADIX
    lanes = min(128, chunk, rows)
    sub = 8

    def where_is(n, start):
        source, first = divmod(n * chunk + start, rows)
        return source, slice(first, first + lanes)

    def step_forward(index, carry):
        at = pl.ds(pl.multiple_of(index * sub, sub), sub)
        for start in range(0, chunk, lanes):
            values = []
            for n in range(RADIX):
                source, span = where_is(n, start)
                values.append((data_ref[group, source, 0, at, span], data_ref[group, source, 1, at, span]))
            for k, (real, imag) in enumerate(complex_fft(values, -1.0)):
                if k > 0:
                    c = tw_ref[0, k : k + 1, start : start + lanes]
                    s = tw_ref[1, k : k + 1, start : start + lanes]
                    real, imag = real * c + imag * s, imag * c - real * s
                work_ref[k, at, start : start + lanes] = real
                work_ref[k, at, chunk + start : chunk + start + lanes] = imag
        return carry

    lax.fori_loop(0, cols // sub, step_forward, 0)
    radius = cutoff_ref[0]
    limit = radius * radius
    fx2 = fx2_ref[position, group, :, 0:1]
    dims = (((1,), (0,)), ((), ()))
    batch = 4

    def step_matmul(index, carry):
        span = pl.ds(index * batch, batch)
        values = work_ref[span].reshape(batch * cols, 2 * chunk)
        spectrum = product(split(values), (fwd_ref[0], fwd_ref[1]), dims)
        width = spectrum.shape[1]
        spectrum = spectrum.reshape(batch, cols, width)
        fy2 = fy2_ref[span]
        low = jnp.where(fx2[None] + fy2 < limit, spectrum, 0.0).reshape(batch * cols, width)
        back = product(split(low), (inv_ref[0], inv_ref[1]), dims)
        work_ref[span] = back.reshape(batch, cols, 2 * chunk)
        return carry

    lax.fori_loop(0, RADIX // batch, step_matmul, 0)

    def step_inverse(index, carry):
        at = pl.ds(pl.multiple_of(index * sub, sub), sub)
        for start in range(0, chunk, lanes):
            values = []
            for k in range(RADIX):
                real = work_ref[k, at, start : start + lanes]
                imag = work_ref[k, at, chunk + start : chunk + start + lanes]
                if k > 0:
                    c = tw_ref[0, k : k + 1, start : start + lanes]
                    s = tw_ref[1, k : k + 1, start : start + lanes]
                    real, imag = real * c - imag * s, imag * c + real * s
                values.append((real, imag))
            for n, (real, imag) in enumerate(complex_fft(values, 1.0)):
                source, span = where_is(n, start)
                out_ref[group, source, 0, at, span] = real
                out_ref[group, source, 1, at, span] = imag
        return carry

    lax.fori_loop(0, cols // sub, step_inverse, 0)


def exchange(
    shards, cutoff_ref, image_hbm, row_ref, tw_ref, fx2_ref, fy2_ref, fwd_ref, inv_ref, out_ref,
    high_ref, low_ref, sent_ref, held_ref, work_ref, back_ref, send_sem, recv_sem, back_send, back_recv, own_sem, image_ref, slab_sem,
):
    groups, _, _, cols, rows = held_ref.shape
    per = shards // UNITS
    me = lax.axis_index("row")

    def partner(step):
        return lax.rem(me + step, shards)

    def forward_copy(group, step):
        dest = partner(step)
        return pltpu.make_async_remote_copy(
            src_ref=sent_ref.at[step, group],
            dst_ref=held_ref.at[group, me],
            send_sem=send_sem.at[group, step],
            recv_sem=recv_sem.at[group, step],
            device_id={"row": dest},
            device_id_type=pl.DeviceIdType.MESH,
        )

    def back_copy(group, step):
        dest = partner(step)
        return pltpu.make_async_remote_copy(
            src_ref=back_ref.at[group, dest],
            dst_ref=out_ref.at[me, group],
            send_sem=back_send.at[group, step],
            recv_sem=back_recv.at[group, step],
            device_id={"row": dest},
            device_id_type=pl.DeviceIdType.MESH,
        )

    def own_copy(group):
        return pltpu.make_async_copy(back_ref.at[group, me], out_ref.at[me, group], own_sem.at[group])

    def every(function):
        def loop(step, carry):
            function(step)
            return carry

        lax.fori_loop(1, shards, loop, 0)

    slabs = slab_sem.shape[0]

    def slab_copy(slab):
        span = pl.ds(slab * (rows // slabs), rows // slabs)
        return pltpu.make_async_copy(image_hbm.at[span], image_ref.at[span], slab_sem.at[slab])

    for slab in range(slabs):
        slab_copy(slab).start()
    barrier = pltpu.get_barrier_semaphore()
    every(
        lambda step: pl.semaphore_signal(
            barrier, inc=1, device_id={"row": partner(step)}, device_id_type=pl.DeviceIdType.MESH
        )
    )
    rows_forward(image_ref, slab_copy, slabs, tw_ref, high_ref, low_ref)
    pl.semaphore_wait(barrier, shards - 1)

    def columns_of(dest):
        unit, part = dest // per, lax.rem(dest, per)
        which = jnp.minimum(unit, 1)
        values = product(
            (row_ref[which, 0, part], row_ref[which, 1, part]),
            (high_ref[unit], low_ref[unit]),
            (((1,), (1,)), ((), ())),
        )
        return values.reshape(groups, 2, cols, rows)

    def produce(step):
        sent_ref[step] = columns_of(partner(step))
        forward_copy(0, step).start()

    every(produce)
    for group in range(1, groups):
        every(lambda step: forward_copy(group, step).start())
    own = columns_of(me)
    for group in range(groups):
        held_ref[group, me] = own[group]

    def filter_group(group, carry):
        every(lambda step: forward_copy(group, step).wait_recv())
        columns_filter(
            group, me, cutoff_ref, held_ref, fx2_ref, fy2_ref, fwd_ref, inv_ref, tw_ref, back_ref, work_ref
        )
        every(lambda step: back_copy(group, step).start())
        own_copy(group).start()
        return carry

    lax.fori_loop(0, groups, filter_group, 0)

    def finish(group, carry):
        every(lambda step: forward_copy(group, step).wait_send())
        every(lambda step: back_copy(group, step).wait())
        own_copy(group).wait()
        return carry

    lax.fori_loop(0, groups, finish, 0)


def rows_inverse(data_ref, image_ref, table_ref, tw_ref, out_ref, work_ref):
    rows, length = image_ref.shape
    chunk = length // RADIX
    lanes = min(128, chunk)
    sub = 8
    dims = (((1,), (0,)), ((), ()))
    work_ref[0] = product(split(data_ref[0].T), (table_ref[0, 0], table_ref[0, 1]), dims)
    rest = jnp.concatenate([data_ref[unit].T for unit in range(1, UNITS)], axis=0)
    turned = product(split(rest), (table_ref[1, 0], table_ref[1, 1]), dims)
    work_ref[1:] = turned.reshape(UNITS - 1, rows, 2 * chunk)

    def step(index, carry):
        at = pl.ds(pl.multiple_of(index * sub, sub), sub)
        for start in range(0, chunk, lanes):
            freqs = [None] * (UNITS + 1)
            for unit in range(UNITS):
                real = work_ref[unit, at, start : start + lanes]
                imag = work_ref[unit, at, chunk + start : chunk + start + lanes]
                if unit == 0:
                    freqs[0], freqs[UNITS] = (real, None), (imag, None)
                else:
                    c = tw_ref[0, unit : unit + 1, start : start + lanes]
                    s = tw_ref[1, unit : unit + 1, start : start + lanes]
                    freqs[unit] = (real * c - imag * s, imag * c + real * s)
            for n, low in enumerate(real_inverse(freqs, RADIX)):
                span = slice(n * chunk + start, n * chunk + start + lanes)
                out_ref[at, span] = image_ref[at, span] - low
        return carry

    lax.fori_loop(0, rows // sub, step, 0)


def whole(shape):
    return pl.BlockSpec(shape, lambda *_: (0,) * len(shape))


def body(image, cutoff):
    rows_local, width = image.shape
    shards = lax.axis_size("row")
    height = rows_local * shards
    band = 3 * width // 8
    kept = band // UNITS
    half = kept // 2
    cols = band // shards
    per = shards // UNITS
    chunk = width // RADIX
    forward0, forward, inverse0, inverse = frequency_table(width, band)
    part = math.gcd(cols, 64)
    groups = cols // part
    order = np.arange(2 * kept).reshape(2, per, groups, part).transpose(1, 2, 0, 3).reshape(-1)
    row_forward = np.stack([table_halves(forward0.T[order]), table_halves(forward.T[order])])
    row_forward = row_forward.reshape(2, 2, per, 2 * cols, 2 * chunk)
    row_inverse = np.stack([table_halves(inverse0[order]), table_halves(inverse[order])])
    col_forward = table_halves(forward)
    col_inverse = table_halves(inverse / (width * height))
    tw = twiddles(width)
    steps = np.arange(-half, half)
    fy = np.arange(RADIX)[:, None] + RADIX * np.concatenate([steps, steps])[None, :]
    fy2 = (fy * fy).astype(np.int32)[:, None, :]
    first = np.arange(half)
    fx = np.concatenate(
        [RADIX * first, UNITS + RADIX * first] + [unit + RADIX * steps for unit in range(1, UNITS)]
    )
    fx2 = np.broadcast_to((fx * fx).reshape(shards, groups, part, 1), (shards, groups, part, 128)).astype(np.int32)

    vmem = pl.BlockSpec(memory_space=pltpu.VMEM)
    returned = pl.pallas_call(
        functools.partial(exchange, shards),
        out_shape=jax.ShapeDtypeStruct((shards, groups, 2, part, rows_local), jnp.float32),
        in_specs=[pl.BlockSpec(memory_space=pltpu.SMEM), pl.BlockSpec(memory_space=pl.ANY)] + [vmem] * 6,
        out_specs=pl.BlockSpec(memory_space=pl.ANY),
        scratch_shapes=[
            pltpu.VMEM((UNITS, rows_local, 2 * chunk), jnp.bfloat16),
            pltpu.VMEM((UNITS, rows_local, 2 * chunk), jnp.bfloat16),
            pltpu.VMEM((shards, groups, 2, part, rows_local), jnp.float32),
            pltpu.VMEM((groups, shards, 2, part, rows_local), jnp.float32),
            pltpu.VMEM((RADIX, part, 2 * chunk), jnp.float32),
            pltpu.VMEM((groups, shards, 2, part, rows_local), jnp.float32),
            pltpu.SemaphoreType.DMA((groups, shards)),
            pltpu.SemaphoreType.DMA((groups, shards)),
            pltpu.SemaphoreType.DMA((groups, shards)),
            pltpu.SemaphoreType.DMA((groups, shards)),
            pltpu.SemaphoreType.DMA((groups,)),
            pltpu.VMEM((rows_local, width), jnp.float32),
            pltpu.SemaphoreType.DMA((math.gcd(rows_local // 16, 4),)),
        ],
        compiler_params=pltpu.CompilerParams(
            vmem_limit_bytes=VMEM, collective_id=0, has_side_effects=True
        ),
    )(cutoff, image, row_forward, tw, fx2, fy2, col_forward, col_inverse)
    params = pltpu.CompilerParams(vmem_limit_bytes=VMEM)
    block = min(128, rows_local)
    return pl.pallas_call(
        rows_inverse,
        grid=(rows_local // block,),
        out_shape=jax.ShapeDtypeStruct((rows_local, width), jnp.float32),
        in_specs=[
            pl.BlockSpec((UNITS, 2 * kept, block), lambda i: (0, 0, i)),
            pl.BlockSpec((block, width), lambda i: (i, 0)),
            whole(row_inverse.shape),
            whole(tw.shape),
        ],
        out_specs=pl.BlockSpec((block, width), lambda i: (i, 0)),
        scratch_shapes=[pltpu.VMEM((UNITS, block, 2 * chunk), jnp.float32)],
        compiler_params=params,
    )(returned.reshape(UNITS, 2 * kept, rows_local), image, row_inverse, tw)


def solution(mesh):
    return jax.shard_map(
        body,
        mesh=mesh,
        in_specs=(P(("sec", "row"), None), P("sec")),
        out_specs=P(("sec", "row"), None),
        check_vma=False,
    )
```
